32 devices in a mesh: dp: 2 (over core), seq: 16 (over z, y, x).
Axes of the slice: x: 2, y: 2, z: 4, core: 2. Of those that a mesh axis runs over, the one named last changes fastest.
Arguments:
- inputs: bfloat16 [2, 8192, 768], P('dp', 'seq'), may hold values from -6 to 6
- cotangent: bfloat16 [2, 8192, 768], P('dp', 'seq'), may hold values from -1.5 to 1.5
- factor_one: bfloat16 [16, 512, 512], P('seq'), may hold values from -0.25 to 0.25
- factor_two: bfloat16 [512, 16, 16], P('seq'), may hold values from -1.5 to 1.5
- up_weight: bfloat16 [2, 384, 1536], P(None, None, 'dp'), may hold values from -0.3125 to 0.3125
- down_weight: bfloat16 [2, 1536, 384], P(None, 'dp'), may hold values from -0.15625 to 0.15625
Outputs:
- outputs: bfloat16 [2, 8192, 768], P('dp', 'seq')
- grad_inputs: bfloat16 [2, 8192, 768], P('dp', 'seq')
- grad_factor_one: float32 [16, 512, 512], P('seq', 'dp')
- grad_factor_two: float32 [512, 16, 16], P('seq', 'dp')
The draws below stay inside these ranges and needn't reach their ends.
All inputs are finite; a program needn't handle non-finite values.
Results may differ from the reference program's by a relative error of at most 0.0066.
Values may be sent and summed in bfloat16 or wider, within the bound.
A program may use at most 64 MiB of HBM per device.

```python
import jax
import jax.numpy as jnp
from jax import lax

BLOCK = 512
GROUP_CH = 384
GROUPS = 2
GROUP_HID = 1536
BLOCKS = 16
CHANNELS = 768
SEQLEN = 8192
N_DP = 2


def shard_levels(own_key, dims, split, low, largest):
    gain, own = 1.0, jax.random.fold_in(own_key, 6)
    for position, parts in split:
        steps = jnp.exp(jax.random.uniform(jax.random.fold_in(own, position), (parts,), jnp.float32, low / len(split), largest / len(split)))
        gain = gain * jnp.repeat(steps, dims[position] // parts).reshape([-1 if axis == position else 1 for axis in range(len(dims))])
    return gain


def centred(own_key, shape, deviation, most, cuts=(), kind=jnp.bfloat16):
    loudness = shard_levels(own_key, shape, cuts, -0.22, 0.18) if cuts else 1.0
    array = jax.random.normal(own_key, shape, jnp.float32) * deviation * loudness
    return jnp.minimum(jnp.maximum(array, -most), most).astype(kind)


def setup_inputs(seed: int = 0) -> dict:
    arg_keys = jax.random.split(jax.random.key(seed), 7)
    return {
        "inputs": centred(arg_keys[0], (N_DP, SEQLEN, CHANNELS), 1.0, 6.0, ((0, 2), (1, 16))),
        "cotangent": centred(arg_keys[1], (N_DP, SEQLEN, CHANNELS), 0.25, 1.5, ((0, 2), (1, 16))),
        "factor_one": centred(arg_keys[2], (BLOCKS, BLOCK, BLOCK), BLOCK ** -0.5, 0.25, ((0, 16),)),
        "factor_two": centred(arg_keys[3], (BLOCK, BLOCKS, BLOCKS), BLOCKS ** -0.5, 1.5, ((0, 16),)),
        "up_weight": centred(arg_keys[4], (GROUPS, GROUP_CH, GROUP_HID), GROUP_CH ** -0.5, 0.3125, ((2, 2),)),
        "down_weight": centred(arg_keys[5], (GROUPS, GROUP_HID, GROUP_CH), GROUP_HID ** -0.5, 0.15625, ((1, 2),)),
    }


def reference(inputs, cotangent, factor_one, factor_two, up_weight, down_weight):
    first = factor_one.astype(jnp.float32)
    second = factor_two.astype(jnp.float32)
    up_full = up_weight.astype(jnp.float32)
    down_full = down_weight.astype(jnp.float32)

    def one_sequence(carry, pair):
        seq_in, seq_cot = pair
        blocked = seq_in.reshape(BLOCKS, BLOCK, CHANNELS).astype(jnp.float32)
        mixed_one = jnp.einsum('apb,abc->apc', first, blocked).astype(jnp.bfloat16)
        cols_one = mixed_one.astype(jnp.float32).transpose(1, 0, 2)
        mixed_pq = jnp.einsum('pqa,pac->pqc', second, cols_one).astype(jnp.bfloat16)
        mixed_two = mixed_pq.astype(jnp.float32).transpose(1, 0, 2).reshape(SEQLEN, CHANNELS)
        input_f = seq_in.astype(jnp.float32)
        silu_vals, silu_back = jax.vjp(jax.nn.silu, input_f)
        gated = (mixed_two * silu_vals).astype(jnp.bfloat16)
        gated_f = gated.astype(jnp.float32).reshape(SEQLEN, GROUPS, GROUP_CH)
        pre = jnp.einsum('tnc,nch->tnh', gated_f, up_full)
        hidden_act, gelu_back = jax.vjp(jax.nn.gelu, pre)
        hidden = hidden_act.astype(jnp.bfloat16).astype(jnp.float32)
        result = gated_f + jnp.einsum('tnh,nhc->tnc', hidden, down_full)
        result = result.reshape(SEQLEN, CHANNELS).astype(jnp.bfloat16)
        cot_f = seq_cot.astype(jnp.float32).reshape(SEQLEN, GROUPS, GROUP_CH)
        grad_hidden = jnp.einsum('tnc,nhc->tnh', cot_f, down_full)
        grad_pre = gelu_back(grad_hidden)[0].astype(jnp.bfloat16).astype(jnp.float32)
        grad_gated = cot_f + jnp.einsum('tnh,nch->tnc', grad_pre, up_full)
        grad_gated = grad_gated.reshape(SEQLEN, CHANNELS)
        grad_two = (grad_gated * silu_vals).astype(jnp.bfloat16)
        grad_gate_in = silu_back(grad_gated * mixed_two)[0]
        grad_cols = grad_two.astype(jnp.float32).reshape(BLOCKS, BLOCK, CHANNELS).transpose(1, 0, 2)
        term_two = jnp.einsum('pqc,pac->pqa', grad_cols, cols_one)
        grad_one_pa = jnp.einsum('pqa,pqc->pac', second, grad_cols).astype(jnp.bfloat16)
        grad_one = grad_one_pa.astype(jnp.float32).transpose(1, 0, 2)
        term_one = jnp.einsum('apc,abc->apb', grad_one, blocked)
        grad_in = grad_gate_in.reshape(BLOCKS, BLOCK, CHANNELS) + jnp.einsum('apb,apc->abc', first, grad_one)
        grad_in = grad_in.reshape(SEQLEN, CHANNELS).astype(jnp.bfloat16)
        return ((carry[0] + term_one, carry[1] + term_two), (result, grad_in))
    start = (jnp.zeros((BLOCKS, BLOCK, BLOCK), jnp.float32), jnp.zeros((BLOCK, BLOCKS, BLOCKS), jnp.float32))
    sums, stacked = lax.scan(one_sequence, start, (inputs, cotangent))
    return (stacked[0], stacked[1], sums[0], sums[1])
```

```python
import functools

import jax
import jax.numpy as jnp
from jax import lax
from jax.experimental import pallas as pl
from jax.experimental.pallas import tpu as pltpu
from jax.sharding import PartitionSpec as P

MESH = pl.DeviceIdType.MESH
F32 = jnp.float32
BF16 = jnp.bfloat16
GELU_A = 0.7978845608028654
GELU_B = 0.044715
TOK_TILE = 128
ROW_TILE = 256


def dot(a, b):
    return jnp.dot(a, b, preferred_element_type=F32)


def dot_nt(a, b):
    return lax.dot_general(a, b, (((1,), (1,)), ((), ())), preferred_element_type=F32)


def kernel(
    n_seq, n_dp,
    x_ref, cot_ref, f1_ref, f2_ref, up_ref, down_ref,
    out_ref, gin_ref, g1_ref, g2_ref,
    src, dst, up_all, down_all, mix, mix_t, f1_t, sel, perm, gate, t1, t1_in, t2, t2_in,
    send_sem, recv_sem, w_send, w_recv, w_local, r_send, r_recv,
):
    me = lax.axis_index("seq")
    core = lax.axis_index("dp")
    block, channels = x_ref.shape
    groups, _, parts, width = src.shape[1], src.shape[2], src.shape[3], src.shape[4]
    rows_one = t1_in.shape[1]
    rows_two = t2_in.shape[1]

    barrier = pltpu.get_barrier_semaphore()

    def greet_seq(k, carry):
        pl.semaphore_signal(
            barrier, inc=1, device_id={"seq": lax.rem(me + k, n_seq)}, device_id_type=MESH
        )
        return carry

    def greet_dp(k, carry):
        pl.semaphore_signal(
            barrier, inc=1, device_id={"dp": lax.rem(core + k, n_dp)}, device_id_type=MESH
        )
        return carry

    lax.fori_loop(1, n_seq, greet_seq, 0)
    lax.fori_loop(1, n_dp, greet_dp, 0)

    def cols(g):
        return pl.ds(g * width, width)

    def flat(ref, phase, g):
        return ref[phase, g].reshape(block, width)

    def send(phase, g):
        def one(k, carry):
            peer = lax.rem(me + k, n_seq)
            pltpu.make_async_remote_copy(
                src_ref=src.at[phase, g, peer],
                dst_ref=dst.at[phase, g, me],
                send_sem=send_sem.at[phase, g],
                recv_sem=recv_sem.at[phase, g],
                device_id={"seq": peer},
                device_id_type=MESH,
            ).start()
            return carry

        lax.fori_loop(1, n_seq, one, 0)
        dst[phase, g, me] = src[phase, g, me]

    def receive(phase, g):
        span = dst.at[phase, g, pl.ds(0, n_seq - 1)]
        pltpu.make_async_copy(span, span, recv_sem.at[phase, g]).wait()

    def row_loop(total, tile, body):
        def step(i, carry):
            body(pl.ds(pl.multiple_of(i * tile, tile), tile))
            return carry

        lax.fori_loop(0, total // tile, step, 0)

    seq_tile = max(1, ROW_TILE // parts)

    def mul_into(phase, g, left, right):
        def step(i, carry):
            tile = seq_tile * parts
            rows = pl.ds(pl.multiple_of(i * tile, tile), tile)
            value = dot(left[rows, :], right()).astype(BF16)
            src[phase, g, pl.ds(i * seq_tile, seq_tile)] = value.reshape(seq_tile, parts, width)
            return carry

        lax.fori_loop(0, n_seq // seq_tile, step, 0)

    mul_into(0, 0, f1_ref, lambda: x_ref[:, cols(0)])
    pl.semaphore_wait(barrier, n_seq + n_dp - 2)
    send(0, 0)

    def send_weights(k, carry):
        peer = lax.rem(core + k, n_dp)
        for i, (mine, everyone) in enumerate(((up_ref, up_all), (down_ref, down_all))):
            pltpu.make_async_remote_copy(
                src_ref=mine,
                dst_ref=everyone.at[core],
                send_sem=w_send.at[i],
                recv_sem=w_recv.at[i],
                device_id={"dp": peer},
                device_id_type=MESH,
            ).start()
        return carry

    lax.fori_loop(1, n_dp, send_weights, 0)
    own = [
        pltpu.make_async_copy(up_ref, up_all.at[core], w_local.at[0]),
        pltpu.make_async_copy(down_ref, down_all.at[core], w_local.at[1]),
    ]
    for copy in own:
        copy.start()
    for g in range(1, groups):
        mul_into(0, g, f1_ref, lambda: x_ref[:, cols(g)])
        send(0, g)

    def iota(shape, axis):
        return lax.broadcasted_iota(jnp.int32, shape, axis)

    square = (block, block)
    per = n_seq // n_dp
    a_row, a_col = iota((n_seq, block), 0), iota((n_seq, block), 1)
    spread = jnp.where(a_row == a_col // parts, 1.0, 0.0).astype(BF16)
    k_row, k_col = iota((block, 128), 0), iota((block, 128), 1)
    sel[...] = jnp.where(k_row // parts == k_col, 1.0, 0.0).astype(BF16)
    row, col = iota(square, 0), iota(square, 1)
    to_q = (row // (parts * per)) * per + row % per
    to_p = (row // per) % parts
    perm[...] = jnp.where(col == to_q * parts + to_p, 1.0, 0.0).astype(BF16)
    order = jnp.where(col == (row % parts) * n_seq + row // parts, 1.0, 0.0).astype(BF16)
    wide = dot(f2_ref[...], spread).astype(BF16)
    full = dot(order, wide)
    full = jnp.where(row % parts == col % parts, full, 0.0)
    mix[...] = full.astype(BF16)
    mix_t[...] = full.T.astype(BF16)
    f1_t[...] = f1_ref[...].astype(F32).T.astype(BF16)

    for g in range(groups):
        receive(0, g)
        mul_into(1, g, mix, lambda: flat(dst, 0, g))
        send(1, g)

    for copy in own:
        copy.wait()
    for i, everyone in enumerate((up_all, down_all)):
        span = everyone.at[pl.ds(0, n_dp - 1)]
        pltpu.make_async_copy(span, span, w_recv.at[i]).wait()

    tok_seq = max(1, TOK_TILE // parts)

    def mlp(g):
        def step(i, carry):
            tile = tok_seq * parts
            rows = pl.ds(pl.multiple_of(i * tile, tile), tile)
            blocks = pl.ds(i * tok_seq, tok_seq)
            x = x_ref[rows, cols(g)].astype(F32)
            sig = 1.0 / (1.0 + jnp.exp(-x))
            silu = x * sig
            mixed = dst[1, g, blocks].reshape(tile, width).astype(F32)
            gated = (mixed * silu).astype(BF16)
            cot = cot_ref[rows, cols(g)]
            result = gated.astype(F32)
            back = cot.astype(F32)
            for d in range(n_dp):
                up, down = up_all[d, g], down_all[d, g]
                pre = dot(gated, up)
                grad_hidden = dot_nt(cot, down)
                sq = pre * pre
                th = jnp.tanh(pre * (GELU_A + (GELU_A * GELU_B) * sq))
                half = 0.5 + 0.5 * th
                hidden = (pre * half).astype(BF16)
                slope = half + (pre * half) * (1.0 - th) * (
                    GELU_A + (3.0 * GELU_A * GELU_B) * sq
                )
                grad_pre = (grad_hidden * slope).astype(BF16)
                result += dot(hidden, down)
                back += dot_nt(grad_pre, up)
            out_ref[rows, cols(g)] = result.astype(BF16)
            src[2, g, blocks] = (back * silu).astype(BF16).reshape(tok_seq, parts, width)
            gate[rows, cols(g)] = back * mixed * (sig * (1.0 + x * (1.0 - sig)))
            return carry

        lax.fori_loop(0, n_seq // tok_seq, step, 0)

    for g in range(groups):
        receive(1, g)
        mlp(g)
        send(2, g)

    for g in range(groups):
        receive(2, g)
        mul_into(3, g, mix_t, lambda: flat(dst, 2, g))
        send(3, g)

    def term_two(rows):
        total = None
        for g in range(groups):
            grads = dot(perm[rows, :], flat(dst, 2, g)).astype(BF16)
            part = dot_nt(grads, flat(dst, 0, g))
            total = part if total is None else total + part
        start = rows.start
        r = start + iota(total.shape, 0)
        c = iota(total.shape, 1)
        total = jnp.where((r // per) % parts == c % parts, total, 0.0)
        high = total.astype(BF16)
        rest = total - high.astype(F32)
        low = rest.astype(BF16)
        last = (rest - low.astype(F32)).astype(BF16)
        t2[rows, :] = dot(high, sel[...]) + dot(low, sel[...]) + dot(last, sel[...])

    row_loop(block, ROW_TILE, term_two)

    def reduce_start(which, whole, landed, size):
        def one(k, carry):
            peer = lax.rem(core + k, n_dp)
            pltpu.make_async_remote_copy(
                src_ref=whole.at[pl.ds(pl.multiple_of(peer * size, size), size)],
                dst_ref=landed.at[core],
                send_sem=r_send.at[which],
                recv_sem=r_recv.at[which],
                device_id={"dp": peer},
                device_id_type=MESH,
            ).start()
            return carry

        lax.fori_loop(1, n_dp, one, 0)
        landed[core] = whole[pl.ds(pl.multiple_of(core * size, size), size), :]

    def reduce_end(which, whole, landed, size, out):
        span = landed.at[pl.ds(0, n_dp - 1)]
        pltpu.make_async_copy(span, span, r_recv.at[which]).wait()
        total = landed[0]
        for d in range(1, n_dp):
            total += landed[d]
        out[...] = total
        sent = whole.at[pl.ds(0, (n_dp - 1) * size)]
        pltpu.make_async_copy(sent, sent, r_send.at[which]).wait()

    reduce_start(1, t2, t2_in, rows_two)

    for g in range(groups):
        receive(3, g)
        grads = flat(dst, 3, g)
        seqs = x_ref[:, cols(g)]
        if g == 0:
            t1[...] = dot_nt(grads, seqs)
        else:
            t1[...] += dot_nt(grads, seqs)
        if g == groups - 1:
            reduce_start(0, t1, t1_in, rows_one)
        gin_ref[:, cols(g)] = (gate[:, cols(g)] + dot(f1_t[...], grads)).astype(BF16)

    reduce_end(1, t2, t2_in, rows_two, g2_ref)
    reduce_end(0, t1, t1_in, rows_one, g1_ref)
    for i, everyone in enumerate((up_all, down_all)):
        span = everyone.at[pl.ds(0, n_dp - 1)]
        pltpu.make_async_copy(span, span, w_send.at[i]).wait()
    for phase in range(4):
        for g in range(groups):
            span = src.at[phase, g, pl.ds(0, n_seq - 1)]
            pltpu.make_async_copy(span, span, send_sem.at[phase, g]).wait()


def shards(n_seq, n_dp, inputs, cotangent, factor_one, factor_two, up_weight, down_weight):
    _, block, channels = inputs.shape
    groups, width, hid = up_weight.shape
    parts = block // n_seq
    per = n_seq // n_dp
    vmem = pl.BlockSpec(memory_space=pltpu.VMEM)
    anywhere = pl.BlockSpec(memory_space=pl.ANY)
    rows_one, rows_two = block // n_dp, parts * per
    exchange = pltpu.VMEM((4, groups, n_seq, parts, width), BF16)
    flops = 2 * block * block * channels * 6 + 2 * block * width * hid * n_dp * groups * 4
    out, gin, g1, g2 = pl.pallas_call(
        functools.partial(kernel, n_seq, n_dp),
        out_shape=(
            jax.ShapeDtypeStruct((block, channels), BF16),
            jax.ShapeDtypeStruct((block, channels), BF16),
            jax.ShapeDtypeStruct((rows_one, block), F32),
            jax.ShapeDtypeStruct((rows_two, 128), F32),
        ),
        in_specs=[vmem, vmem, vmem, vmem, anywhere, anywhere],
        out_specs=(vmem, vmem, vmem, vmem),
        scratch_shapes=[
            exchange,
            exchange,
            pltpu.VMEM((n_dp, groups, width, hid), BF16),
            pltpu.VMEM((n_dp, groups, hid, width), BF16),
            pltpu.VMEM((block, block), BF16),
            pltpu.VMEM((block, block), BF16),
            pltpu.VMEM((block, block), BF16),
            pltpu.VMEM((block, 128), BF16),
            pltpu.VMEM((block, block), BF16),
            pltpu.VMEM((block, channels), F32),
            pltpu.VMEM((block, block), F32),
            pltpu.VMEM((n_dp, rows_one, block), F32),
            pltpu.VMEM((block, 128), F32),
            pltpu.VMEM((n_dp, rows_two, 128), F32),
            pltpu.SemaphoreType.DMA((4, groups)),
            pltpu.SemaphoreType.DMA((4, groups)),
            pltpu.SemaphoreType.DMA((2,)),
            pltpu.SemaphoreType.DMA((2,)),
            pltpu.SemaphoreType.DMA((2,)),
            pltpu.SemaphoreType.DMA((2,)),
            pltpu.SemaphoreType.DMA((2,)),
        ],
        compiler_params=pltpu.CompilerParams(
            collective_id=0, has_side_effects=True, vmem_limit_bytes=52 * 2**20
        ),
        cost_estimate=pl.CostEstimate(flops=flops, bytes_accessed=2**23, transcendentals=2**21),
    )(
        inputs[0], cotangent[0], factor_one[0],
        factor_two.reshape(block, n_seq), up_weight, down_weight,
    )
    return out[None], gin[None], g1[None], g2[:, :n_seq].reshape(parts, per, n_seq)


def solution(mesh):
    in_specs = (
        P("dp", "seq", None),
        P("dp", "seq", None),
        P("seq", None, None),
        P("seq", None, None),
        P(None, None, "dp"),
        P(None, "dp", None),
    )
    out_specs = (
        P("dp", "seq", None),
        P("dp", "seq", None),
        P("seq", "dp", None),
        P("seq", "dp", None),
    )
    body = functools.partial(shards, mesh.shape["seq"], mesh.shape["dp"])
    return jax.shard_map(body, mesh=mesh, in_specs=in_specs, out_specs=out_specs, check_vma=False)
```

```python
import functools

import jax
import jax.numpy as jnp
from jax import lax
from jax.experimental import pallas as pl
from jax.experimental.pallas import tpu as pltpu
from jax.sharding import PartitionSpec as P

MESH = pl.DeviceIdType.MESH
F32 = jnp.float32
BF16 = jnp.bfloat16
GELU_A = 0.7978845608028654
GELU_B = 0.044715
TOK_TILE = 128
ROW_TILE = 256


def dot(a, b):
    return jnp.dot(a, b, preferred_element_type=F32)


def dot_nt(a, b):
    return lax.dot_general(a, b, (((1,), (1,)), ((), ())), preferred_element_type=F32)


def kernel(
    n_seq, n_dp,
    x_in, cot_in, f1_in, f2_ref, up_ref, down_ref,
    out_ref, gin_ref, g1_ref, g2_ref,
    x_ref, cot_ref, f1_ref, src, dst, up_all, down_all, mix, mix_t, f1_t, gate, t1, t1_in, t2, t2_in,
    send_sem, recv_sem, w_send, w_recv, w_local, in_sem, r_send, r_recv,
):
    me = lax.axis_index("seq")
    core = lax.axis_index("dp")
    block, channels = x_ref.shape
    groups, _, parts, width = src.shape[1], src.shape[2], src.shape[3], src.shape[4]
    rows_one = t1_in.shape[1]
    rows_two = t2_in.shape[1]
    loads = [
        pltpu.make_async_copy(x_in, x_ref, in_sem.at[0]),
        pltpu.make_async_copy(f1_in, f1_ref, in_sem.at[1]),
        pltpu.make_async_copy(cot_in, cot_ref, in_sem.at[2]),
    ]
    loads[0].start()
    loads[1].start()

    barrier = pltpu.get_barrier_semaphore()

    def greet_seq(k, carry):
        pl.semaphore_signal(
            barrier, inc=1, device_id={"seq": lax.rem(me + k, n_seq)}, device_id_type=MESH
        )
        return carry

    def greet_dp(k, carry):
        pl.semaphore_signal(
            barrier, inc=1, device_id={"dp": lax.rem(core + k, n_dp)}, device_id_type=MESH
        )
        return carry

    lax.fori_loop(1, n_seq, greet_seq, 0)
    lax.fori_loop(1, n_dp, greet_dp, 0)

    def cols(g):
        return pl.ds(g * width, width)

    def flat(ref, phase, g):
        return ref[phase, g].reshape(block, width)

    def send(phase, g):
        def one(k, carry):
            step = (k + 1) // 2
            shift = n_seq // 2 + jnp.where(k % 2 == 1, step, -step)
            peer = lax.rem(me + shift, n_seq)
            pltpu.make_async_remote_copy(
                src_ref=src.at[phase, g, peer],
                dst_ref=dst.at[phase, g, me],
                send_sem=send_sem.at[phase, g],
                recv_sem=recv_sem.at[phase, g],
                device_id={"seq": peer},
                device_id_type=MESH,
            ).start()
            return carry

        lax.fori_loop(0, n_seq - 1, one, 0)
        dst[phase, g, me] = src[phase, g, me]

    def receive(phase, g):
        span = dst.at[phase, g, pl.ds(0, n_seq - 1)]
        pltpu.make_async_copy(span, span, recv_sem.at[phase, g]).wait()

    def row_loop(total, tile, body):
        def step(i, carry):
            body(pl.ds(pl.multiple_of(i * tile, tile), tile))
            return carry

        lax.fori_loop(0, total // tile, step, 0)

    seq_tile = max(1, ROW_TILE // parts)

    def mul_into(phase, g, left, right):
        def step(i, carry):
            tile = seq_tile * parts
            rows = pl.ds(pl.multiple_of(i * tile, tile), tile)
            value = dot(left[rows, :], right()).astype(BF16)
            src[phase, g, pl.ds(i * seq_tile, seq_tile)] = value.reshape(seq_tile, parts, width)
            return carry

        lax.fori_loop(0, n_seq // seq_tile, step, 0)

    loads[0].wait()
    loads[1].wait()
    mul_into(0, 0, f1_ref, lambda: x_ref[:, cols(0)])
    pl.semaphore_wait(barrier, n_seq + n_dp - 2)
    send(0, 0)

    def send_weights(k, carry):
        peer = lax.rem(core + k, n_dp)
        for i, (mine, everyone) in enumerate(((up_ref, up_all), (down_ref, down_all))):
            pltpu.make_async_remote_copy(
                src_ref=mine,
                dst_ref=everyone.at[core],
                send_sem=w_send.at[i],
                recv_sem=w_recv.at[i],
                device_id={"dp": peer},
                device_id_type=MESH,
            ).start()
        return carry

    lax.fori_loop(1, n_dp, send_weights, 0)
    own = [
        pltpu.make_async_copy(up_ref, up_all.at[core], w_local.at[0]),
        pltpu.make_async_copy(down_ref, down_all.at[core], w_local.at[1]),
    ]
    for copy in own + loads[2:]:
        copy.start()
    for g in range(1, groups):
        mul_into(0, g, f1_ref, lambda: x_ref[:, cols(g)])
        send(0, g)

    def iota(shape, axis):
        return lax.broadcasted_iota(jnp.int32, shape, axis)

    tiles = jnp.where(iota((parts, block), 0) == iota((parts, block), 1) % parts, 1.0, 0.0)
    tiles_low = tiles.astype(BF16)
    own_a = iota((n_seq, block), 0) == iota((n_seq, block), 1) // parts

    def build(q, carry):
        wide = dot(f2_ref[pl.ds(pl.multiple_of(q * n_seq, n_seq), n_seq), :], tiles_low)
        line = jnp.sum(jnp.where(own_a, wide, 0.0), axis=0, keepdims=True)
        t1[pl.ds(pl.multiple_of(q * parts, parts), parts), :] = tiles * line
        return carry

    lax.fori_loop(0, n_seq, build, 0)
    mix[...] = t1[...].astype(BF16)
    mix_t[...] = t1[...].T.astype(BF16)
    f1_t[...] = f1_ref[...].astype(F32).T.astype(BF16)

    for g in range(groups):
        receive(0, g)
        mul_into(1, g, mix, lambda: flat(dst, 0, g))
        send(1, g)

    for copy in own + loads[2:]:
        copy.wait()
    for i, everyone in enumerate((up_all, down_all)):
        span = everyone.at[pl.ds(0, n_dp - 1)]
        pltpu.make_async_copy(span, span, w_recv.at[i]).wait()

    tok_seq = max(1, TOK_TILE // parts)

    def mlp(g):
        def step(i, carry):
            tile = tok_seq * parts
            rows = pl.ds(pl.multiple_of(i * tile, tile), tile)
            blocks = pl.ds(i * tok_seq, tok_seq)
            x = x_ref[rows, cols(g)].astype(F32)
            sig = 1.0 / (1.0 + jnp.exp(-x))
            silu = x * sig
            mixed = dst[1, g, blocks].reshape(tile, width).astype(F32)
            gated = (mixed * silu).astype(BF16)
            cot = cot_ref[rows, cols(g)]
            result = gated.astype(F32)
            back = cot.astype(F32)
            for d in range(n_dp):
                up, down = up_all[d, g], down_all[d, g]
                pre = dot(gated, up)
                grad_hidden = dot_nt(cot, down)
                sq = pre * pre
                th = jnp.tanh(pre * (GELU_A + (GELU_A * GELU_B) * sq))
                half = 0.5 + 0.5 * th
                hidden = (pre * half).astype(BF16)
                slope = half + (pre * half) * (1.0 - th) * (
                    GELU_A + (3.0 * GELU_A * GELU_B) * sq
                )
                grad_pre = (grad_hidden * slope).astype(BF16)
                result += dot(hidden, down)
                back += dot_nt(grad_pre, up)
            out_ref[rows, cols(g)] = result.astype(BF16)
            src[2, g, blocks] = (back * silu).astype(BF16).reshape(tok_seq, parts, width)
            gate[rows, cols(g)] = back * mixed * (sig * (1.0 + x * (1.0 - sig)))
            return carry

        lax.fori_loop(0, n_seq // tok_seq, step, 0)

    for g in range(groups):
        receive(1, g)
        mlp(g)
        send(2, g)

    for g in range(groups):
        receive(2, g)
        mul_into(3, g, mix_t, lambda: flat(dst, 2, g))
        send(3, g)

    same = iota((parts, block), 0) == iota((parts, block), 1) % parts
    for tile in range(0, n_seq, seq_tile):
        rows = pl.ds(tile, seq_tile)
        total = None
        for g in range(groups):
            grads = dst[2, g, rows].reshape(seq_tile * parts, width)
            part = dot_nt(grads, flat(dst, 0, g))
            total = part if total is None else total + part
        total = jnp.where(same[None], total.reshape(seq_tile, parts, block), 0.0)
        t2[rows, :] = jnp.sum(total, axis=1)

    def reduce_start(which, whole, landed, size):
        def one(k, carry):
            peer = lax.rem(core + k, n_dp)
            pltpu.make_async_remote_copy(
                src_ref=whole.at[pl.ds(pl.multiple_of(peer * size, size), size)],
                dst_ref=landed.at[core],
                send_sem=r_send.at[which],
                recv_sem=r_recv.at[which],
                device_id={"dp": peer},
                device_id_type=MESH,
            ).start()
            return carry

        lax.fori_loop(1, n_dp, one, 0)
        landed[core] = whole[pl.ds(pl.multiple_of(core * size, size), size), :]

    def reduce_end(which, whole, landed, size, out):
        span = landed.at[pl.ds(0, n_dp - 1)]
        pltpu.make_async_copy(span, span, r_recv.at[which]).wait()
        total = landed[0]
        for d in range(1, n_dp):
            total += landed[d]
        out[...] = total
        sent = whole.at[pl.ds(0, (n_dp - 1) * size)]
        pltpu.make_async_copy(sent, sent, r_send.at[which]).wait()

    reduce_start(1, t2, t2_in, rows_two)

    for g in range(groups):
        receive(3, g)
        grads = flat(dst, 3, g)
        seqs = x_ref[:, cols(g)]
        if g == 0:
            t1[...] = dot_nt(grads, seqs)
        else:
            t1[...] += dot_nt(grads, seqs)
        if g == groups - 1:
            reduce_start(0, t1, t1_in, rows_one)
        gin_ref[:, cols(g)] = (gate[:, cols(g)] + dot(f1_t[...], grads)).astype(BF16)

    reduce_end(1, t2, t2_in, rows_two, g2_ref)
    reduce_end(0, t1, t1_in, rows_one, g1_ref)
    for i, everyone in enumerate((up_all, down_all)):
        span = everyone.at[pl.ds(0, n_dp - 1)]
        pltpu.make_async_copy(span, span, w_send.at[i]).wait()
    for phase in range(4):
        for g in range(groups):
            span = src.at[phase, g, pl.ds(0, n_seq - 1)]
            pltpu.make_async_copy(span, span, send_sem.at[phase, g]).wait()


def finish(out_ref, gin_ref, g1_ref, g2_ref, out, gin, g1, g2, sem):
    copies = [
        pltpu.make_async_copy(a, b, sem.at[i])
        for i, (a, b) in enumerate(((out_ref, out), (gin_ref, gin), (g1_ref, g1)))
    ]
    for copy in copies:
        copy.start()
    _, n_a, parts = g2.shape
    for a in range(n_a):
        g2[:, a, :] = g2_ref[:, a * parts:(a + 1) * parts]
    for copy in copies:
        copy.wait()


def shards(n_seq, n_dp, inputs, cotangent, factor_one, factor_two, up_weight, down_weight):
    _, block, channels = inputs.shape
    groups, width, hid = up_weight.shape
    parts = block // n_seq
    per = n_seq // n_dp
    vmem = pl.BlockSpec(memory_space=pltpu.VMEM)
    hbm = pl.BlockSpec(memory_space=pltpu.HBM)
    rows_one, rows_two = block // n_dp, per
    exchange = pltpu.VMEM((4, groups, n_seq, parts, width), BF16)
    flops = 2 * block * block * channels * 6 + 2 * block * width * hid * n_dp * groups * 4
    out, gin, g1, g2 = pl.pallas_call(
        functools.partial(kernel, n_seq, n_dp),
        out_shape=(
            pltpu.VMEM((block, channels), BF16),
            pltpu.VMEM((block, channels), BF16),
            pltpu.VMEM((rows_one, block), F32),
            pltpu.VMEM((rows_two, block), F32),
        ),
        in_specs=[hbm, hbm, hbm, vmem, hbm, hbm],
        out_specs=(vmem, vmem, vmem, vmem),
        scratch_shapes=[
            pltpu.VMEM((block, channels), BF16),
            pltpu.VMEM((block, channels), BF16),
            pltpu.VMEM((block, block), BF16),
            exchange,
            exchange,
            pltpu.VMEM((n_dp, groups, width, hid), BF16),
            pltpu.VMEM((n_dp, groups, hid, width), BF16),
            pltpu.VMEM((block, block), BF16),
            pltpu.VMEM((block, block), BF16),
            pltpu.VMEM((block, block), BF16),
            pltpu.VMEM((block, channels), F32),
            pltpu.VMEM((block, block), F32),
            pltpu.VMEM((n_dp, rows_one, block), F32),
            pltpu.VMEM((n_seq, block), F32),
            pltpu.VMEM((n_dp, rows_two, block), F32),
            pltpu.SemaphoreType.DMA((4, groups)),
            pltpu.SemaphoreType.DMA((4, groups)),
            pltpu.SemaphoreType.DMA((2,)),
            pltpu.SemaphoreType.DMA((2,)),
            pltpu.SemaphoreType.DMA((2,)),
            pltpu.SemaphoreType.DMA((3,)),
            pltpu.SemaphoreType.DMA((2,)),
            pltpu.SemaphoreType.DMA((2,)),
        ],
        compiler_params=pltpu.CompilerParams(
            collective_id=0, has_side_effects=True, vmem_limit_bytes=58 * 2**20
        ),
        cost_estimate=pl.CostEstimate(flops=flops, bytes_accessed=2**23, transcendentals=2**21),
    )(
        inputs[0], cotangent[0], factor_one[0],
        factor_two.transpose(1, 2, 0).reshape(n_seq * n_seq, parts), up_weight, down_weight,
    )
    out, gin, g1, g2 = pl.pallas_call(
        finish,
        out_shape=(
            jax.ShapeDtypeStruct((block, channels), BF16),
            jax.ShapeDtypeStruct((block, channels), BF16),
            jax.ShapeDtypeStruct((rows_one, block), F32),
            jax.ShapeDtypeStruct((per, n_seq, parts), F32),
        ),
        in_specs=[vmem, vmem, vmem, vmem],
        out_specs=(hbm, hbm, hbm, vmem),
        scratch_shapes=[pltpu.SemaphoreType.DMA((3,))],
        compiler_params=pltpu.CompilerParams(vmem_limit_bytes=8 * 2**20),
    )(out, gin, g1, g2)
    return out[None], gin[None], g1[None], g2.transpose(2, 0, 1)


def solution(mesh):
    in_specs = (
        P("dp", "seq", None),
        P("dp", "seq", None),
        P("seq", None, None),
        P("seq", None, None),
        P(None, None, "dp"),
        P(None, "dp", None),
    )
    out_specs = (
        P("dp", "seq", None),
        P("dp", "seq", None),
        P("seq", "dp", None),
        P("seq", "dp", None),
    )
    body = functools.partial(shards, mesh.shape["seq"], mesh.shape["dp"])
    return jax.shard_map(body, mesh=mesh, in_specs=in_specs, out_specs=out_specs, check_vma=False)
```

```python
import functools

import jax
import jax.numpy as jnp
from jax import lax
from jax.experimental import pallas as pl
from jax.experimental.pallas import tpu as pltpu
from jax.sharding import PartitionSpec as P

MESH = pl.DeviceIdType.MESH
F32 = jnp.float32
BF16 = jnp.bfloat16
GELU_A = 0.7978845608028654
GELU_B = 0.044715
TOK_TILE = 128
ROW_TILE = 256


def dot(a, b):
    return jnp.dot(a, b, preferred_element_type=F32)


def dot_nt(a, b):
    return lax.dot_general(a, b, (((1,), (1,)), ((), ())), preferred_element_type=F32)


def kernel(
    n_seq, n_dp,
    x_in, cot_in, f1_in, f2_ref, up_ref, down_ref,
    out_ref, gin_ref, g1_ref, g2_ref,
    x_ref, cot_ref, f1_ref, src, dst, up_all, down_all, mix, mix_t, f1_t, gate, t1, x_all, g_all, t2, t2_in,
    send_sem, recv_sem, w_send, w_recv, w_local, in_sem, r_send, r_recv,
):
    me = lax.axis_index("seq")
    core = lax.axis_index("dp")
    block, channels = x_ref.shape
    groups, _, parts, width = src.shape[1], src.shape[2], src.shape[3], src.shape[4]
    rows_one = g1_ref.shape[0]
    rows_two = t2_in.shape[1]
    per = n_seq // n_dp
    loads = [
        pltpu.make_async_copy(x_in, x_ref, in_sem.at[0]),
        pltpu.make_async_copy(f1_in, f1_ref, in_sem.at[1]),
        pltpu.make_async_copy(cot_in, cot_ref, in_sem.at[2]),
    ]
    loads[0].start()
    loads[1].start()

    barrier = pltpu.get_barrier_semaphore()

    def greet_seq(k, carry):
        pl.semaphore_signal(
            barrier, inc=1, device_id={"seq": lax.rem(me + k, n_seq)}, device_id_type=MESH
        )
        return carry

    def greet_dp(k, carry):
        pl.semaphore_signal(
            barrier, inc=1, device_id={"dp": lax.rem(core + k, n_dp)}, device_id_type=MESH
        )
        return carry

    lax.fori_loop(1, n_seq, greet_seq, 0)
    lax.fori_loop(1, n_dp, greet_dp, 0)

    def cols(g):
        return pl.ds(g * width, width)

    def flat(ref, phase, g):
        return ref[phase, g].reshape(block, width)

    def send(phase, g):
        def one(k, carry):
            step = (k + 1) // 2
            shift = n_seq // 2 + jnp.where(k % 2 == 1, step, -step)
            peer = lax.rem(me + shift, n_seq)
            pltpu.make_async_remote_copy(
                src_ref=src.at[phase, g, peer],
                dst_ref=dst.at[phase, g, me],
                send_sem=send_sem.at[phase, g],
                recv_sem=recv_sem.at[phase, g],
                device_id={"seq": peer},
                device_id_type=MESH,
            ).start()
            return carry

        lax.fori_loop(0, n_seq - 1, one, 0)
        dst[phase, g, me] = src[phase, g, me]

    def receive(phase, g):
        span = dst.at[phase, g, pl.ds(0, n_seq - 1)]
        pltpu.make_async_copy(span, span, recv_sem.at[phase, g]).wait()

    def row_loop(total, tile, body):
        def step(i, carry):
            body(pl.ds(pl.multiple_of(i * tile, tile), tile))
            return carry

        lax.fori_loop(0, total // tile, step, 0)

    seq_tile = max(1, ROW_TILE // parts)

    def mul_into(phase, g, left, right):
        def step(i, carry):
            tile = seq_tile * parts
            rows = pl.ds(pl.multiple_of(i * tile, tile), tile)
            value = dot(left[rows, :], right()).astype(BF16)
            src[phase, g, pl.ds(i * seq_tile, seq_tile)] = value.reshape(seq_tile, parts, width)
            return carry

        lax.fori_loop(0, n_seq // seq_tile, step, 0)

    loads[0].wait()
    loads[1].wait()
    mul_into(0, 0, f1_ref, lambda: x_ref[:, cols(0)])
    pl.semaphore_wait(barrier, n_seq + n_dp - 2)
    send(0, 0)

    def send_weights(k, carry):
        peer = lax.rem(core + k, n_dp)
        for i, (mine, everyone) in enumerate(((up_ref, up_all), (down_ref, down_all))):
            pltpu.make_async_remote_copy(
                src_ref=mine,
                dst_ref=everyone.at[core],
                send_sem=w_send.at[i],
                recv_sem=w_recv.at[i],
                device_id={"dp": peer},
                device_id_type=MESH,
            ).start()
        pltpu.make_async_remote_copy(
            src_ref=x_ref,
            dst_ref=x_all.at[core],
            send_sem=r_send.at[0],
            recv_sem=r_recv.at[0],
            device_id={"dp": peer},
            device_id_type=MESH,
        ).start()
        return carry

    lax.fori_loop(1, n_dp, send_weights, 0)
    own = [
        pltpu.make_async_copy(up_ref, up_all.at[core], w_local.at[0]),
        pltpu.make_async_copy(down_ref, down_all.at[core], w_local.at[1]),
    ]
    for copy in own + loads[2:]:
        copy.start()
    for g in range(1, groups):
        mul_into(0, g, f1_ref, lambda: x_ref[:, cols(g)])
        send(0, g)

    def iota(shape, axis):
        return lax.broadcasted_iota(jnp.int32, shape, axis)

    tiles = jnp.where(iota((parts, block), 0) == iota((parts, block), 1) % parts, 1.0, 0.0)
    tiles_low = tiles.astype(BF16)
    own_a = iota((n_seq, block), 0) == iota((n_seq, block), 1) // parts

    def build(q, carry):
        wide = dot(f2_ref[pl.ds(pl.multiple_of(q * n_seq, n_seq), n_seq), :], tiles_low)
        line = jnp.sum(jnp.where(own_a, wide, 0.0), axis=0, keepdims=True)
        t1[pl.ds(pl.multiple_of(q * parts, parts), parts), :] = tiles * line
        return carry

    lax.fori_loop(0, n_seq, build, 0)
    mix[...] = t1[...].astype(BF16)
    mix_t[...] = t1[...].T.astype(BF16)
    f1_t[...] = f1_ref[...].astype(F32).T.astype(BF16)

    for g in range(groups):
        receive(0, g)
        mul_into(1, g, mix, lambda: flat(dst, 0, g))
        send(1, g)

    for copy in own + loads[2:]:
        copy.wait()
    for i, everyone in enumerate((up_all, down_all)):
        span = everyone.at[pl.ds(0, n_dp - 1)]
        pltpu.make_async_copy(span, span, w_recv.at[i]).wait()

    tok_seq = max(1, TOK_TILE // parts)

    def mlp(g):
        def step(i, carry):
            tile = tok_seq * parts
            rows = pl.ds(pl.multiple_of(i * tile, tile), tile)
            blocks = pl.ds(i * tok_seq, tok_seq)
            x = x_ref[rows, cols(g)].astype(F32)
            sig = 1.0 / (1.0 + jnp.exp(-x))
            silu = x * sig
            mixed = dst[1, g, blocks].reshape(tile, width).astype(F32)
            gated = (mixed * silu).astype(BF16)
            cot = cot_ref[rows, cols(g)]
            result = gated.astype(F32)
            back = cot.astype(F32)
            for d in range(n_dp):
                up, down = up_all[d, g], down_all[d, g]
                pre = dot(gated, up)
                grad_hidden = dot_nt(cot, down)
                sq = pre * pre
                th = jnp.tanh(pre * (GELU_A + (GELU_A * GELU_B) * sq))
                half = 0.5 + 0.5 * th
                hidden = (pre * half).astype(BF16)
                slope = half + (pre * half) * (1.0 - th) * (
                    GELU_A + (3.0 * GELU_A * GELU_B) * sq
                )
                grad_pre = (grad_hidden * slope).astype(BF16)
                result += dot(hidden, down)
                back += dot_nt(grad_pre, up)
            out_ref[rows, cols(g)] = result.astype(BF16)
            src[2, g, blocks] = (back * silu).astype(BF16).reshape(tok_seq, parts, width)
            gate[rows, cols(g)] = back * mixed * (sig * (1.0 + x * (1.0 - sig)))
            return carry

        lax.fori_loop(0, n_seq // tok_seq, step, 0)

    for g in range(groups):
        receive(1, g)
        mlp(g)
        send(2, g)

    for g in range(groups):
        receive(2, g)
        mul_into(3, g, mix_t, lambda: flat(dst, 2, g))
        send(3, g)

    same = iota((parts, block), 0) == iota((parts, block), 1) % parts
    for tile in range(0, n_seq, seq_tile):
        rows = pl.ds(tile, seq_tile)
        total = None
        for g in range(groups):
            grads = dst[2, g, rows].reshape(seq_tile * parts, width)
            part = dot_nt(grads, flat(dst, 0, g))
            total = part if total is None else total + part
        total = jnp.where(same[None], total.reshape(seq_tile, parts, block), 0.0)
        t2[rows, :] = jnp.sum(total, axis=1)

    def reduce_start(which, whole, landed, size):
        def one(k, carry):
            peer = lax.rem(core + k, n_dp)
            pltpu.make_async_remote_copy(
                src_ref=whole.at[pl.ds(pl.multiple_of(peer * size, size), size)],
                dst_ref=landed.at[core],
                send_sem=r_send.at[which],
                recv_sem=r_recv.at[which],
                device_id={"dp": peer},
                device_id_type=MESH,
            ).start()
            return carry

        lax.fori_loop(1, n_dp, one, 0)
        landed[core] = whole[pl.ds(pl.multiple_of(core * size, size), size), :]

    def reduce_end(which, whole, landed, size, out):
        span = landed.at[pl.ds(0, n_dp - 1)]
        pltpu.make_async_copy(span, span, r_recv.at[which]).wait()
        total = landed[0]
        for d in range(1, n_dp):
            total += landed[d]
        out[...] = total
        sent = whole.at[pl.ds(0, (n_dp - 1) * size)]
        pltpu.make_async_copy(sent, sent, r_send.at[which]).wait()

    reduce_start(1, t2, t2_in, rows_two)

    reduce_end(1, t2, t2_in, rows_two, g2_ref)
    others = x_all.at[pl.ds(0, n_dp - 1)]
    pltpu.make_async_copy(others, others, r_recv.at[0]).wait()

    def forward(g):
        def one(k, carry):
            peer = lax.rem(core + k, n_dp)
            pltpu.make_async_remote_copy(
                src_ref=dst.at[3, g, pl.ds(peer * per, per)],
                dst_ref=g_all.at[g, core],
                send_sem=r_send.at[2 + g],
                recv_sem=r_recv.at[2 + g],
                device_id={"dp": peer},
                device_id_type=MESH,
            ).start()
            return carry

        lax.fori_loop(1, n_dp, one, 0)

    for g in range(groups):
        receive(3, g)
        forward(g)
        gin_ref[:, cols(g)] = (gate[:, cols(g)] + dot(f1_t[...], flat(dst, 3, g))).astype(BF16)
        mine = dst[3, g, pl.ds(core * per, per)].reshape(rows_one, width)
        part = dot_nt(mine, x_ref[:, cols(g)])
        if g == 0:
            g1_ref[...] = part
        else:
            g1_ref[...] += part
        span = g_all.at[g, pl.ds(0, n_dp - 1)]
        pltpu.make_async_copy(span, span, r_recv.at[2 + g]).wait()
        for k in range(1, n_dp):
            d = lax.rem(core + k, n_dp)
            g1_ref[...] += dot_nt(g_all[g, d].reshape(rows_one, width), x_all[d, :, cols(g)])

    pltpu.make_async_copy(others, others, r_send.at[0]).wait()
    for g in range(groups):
        span = g_all.at[g, pl.ds(0, n_dp - 1)]
        pltpu.make_async_copy(span, span, r_send.at[2 + g]).wait()
    for i, everyone in enumerate((up_all, down_all)):
        span = everyone.at[pl.ds(0, n_dp - 1)]
        pltpu.make_async_copy(span, span, w_send.at[i]).wait()
    for phase in range(4):
        for g in range(groups):
            span = src.at[phase, g, pl.ds(0, n_seq - 1)]
            pltpu.make_async_copy(span, span, send_sem.at[phase, g]).wait()


def finish(out_ref, gin_ref, g1_ref, g2_ref, out, gin, g1, g2, sem):
    copies = [
        pltpu.make_async_copy(a, b, sem.at[i])
        for i, (a, b) in enumerate(((out_ref, out), (gin_ref, gin), (g1_ref, g1)))
    ]
    for copy in copies:
        copy.start()
    _, n_a, parts = g2.shape
    for a in range(n_a):
        g2[:, a, :] = g2_ref[:, a * parts:(a + 1) * parts]
    for copy in copies:
        copy.wait()


def shards(n_seq, n_dp, inputs, cotangent, factor_one, factor_two, up_weight, down_weight):
    _, block, channels = inputs.shape
    groups, width, hid = up_weight.shape
    parts = block // n_seq
    per = n_seq // n_dp
    vmem = pl.BlockSpec(memory_space=pltpu.VMEM)
    hbm = pl.BlockSpec(memory_space=pltpu.HBM)
    rows_one, rows_two = block // n_dp, per
    exchange = pltpu.VMEM((4, groups, n_seq, parts, width), BF16)
    flops = 2 * block * block * channels * 6 + 2 * block * width * hid * n_dp * groups * 4
    out, gin, g1, g2 = pl.pallas_call(
        functools.partial(kernel, n_seq, n_dp),
        out_shape=(
            pltpu.VMEM((block, channels), BF16),
            pltpu.VMEM((block, channels), BF16),
            pltpu.VMEM((rows_one, block), F32),
            pltpu.VMEM((rows_two, block), F32),
        ),
        in_specs=[hbm, hbm, hbm, vmem, hbm, hbm],
        out_specs=(vmem, vmem, vmem, vmem),
        scratch_shapes=[
            pltpu.VMEM((block, channels), BF16),
            pltpu.VMEM((block, channels), BF16),
            pltpu.VMEM((block, block), BF16),
            exchange,
            exchange,
            pltpu.VMEM((n_dp, groups, width, hid), BF16),
            pltpu.VMEM((n_dp, groups, hid, width), BF16),
            pltpu.VMEM((block, block), BF16),
            pltpu.VMEM((block, block), BF16),
            pltpu.VMEM((block, block), BF16),
            pltpu.VMEM((block, channels), F32),
            pltpu.VMEM((block, block), F32),
            pltpu.VMEM((n_dp, block, channels), BF16),
            pltpu.VMEM((groups, n_dp, per, parts, width), BF16),
            pltpu.VMEM((n_seq, block), F32),
            pltpu.VMEM((n_dp, rows_two, block), F32),
            pltpu.SemaphoreType.DMA((4, groups)),
            pltpu.SemaphoreType.DMA((4, groups)),
            pltpu.SemaphoreType.DMA((2,)),
            pltpu.SemaphoreType.DMA((2,)),
            pltpu.SemaphoreType.DMA((2,)),
            pltpu.SemaphoreType.DMA((3,)),
            pltpu.SemaphoreType.DMA((2 + groups,)),
            pltpu.SemaphoreType.DMA((2 + groups,)),
        ],
        compiler_params=pltpu.CompilerParams(
            collective_id=0, has_side_effects=True, vmem_limit_bytes=58 * 2**20
        ),
        cost_estimate=pl.CostEstimate(flops=flops, bytes_accessed=2**23, transcendentals=2**21),
    )(
        inputs[0], cotangent[0], factor_one[0],
        factor_two.transpose(1, 2, 0).reshape(n_seq * n_seq, parts), up_weight, down_weight,
    )
    out, gin, g1, g2 = pl.pallas_call(
        finish,
        out_shape=(
            jax.ShapeDtypeStruct((block, channels), BF16),
            jax.ShapeDtypeStruct((block, channels), BF16),
            jax.ShapeDtypeStruct((rows_one, block), F32),
            jax.ShapeDtypeStruct((per, n_seq, parts), F32),
        ),
        in_specs=[vmem, vmem, vmem, vmem],
        out_specs=(hbm, hbm, hbm, vmem),
        scratch_shapes=[pltpu.SemaphoreType.DMA((3,))],
        compiler_params=pltpu.CompilerParams(vmem_limit_bytes=8 * 2**20),
    )(out, gin, g1, g2)
    return out[None], gin[None], g1[None], g2.transpose(2, 0, 1)


def solution(mesh):
    in_specs = (
        P("dp", "seq", None),
        P("dp", "seq", None),
        P("seq", None, None),
        P("seq", None, None),
        P(None, None, "dp"),
        P(None, "dp", None),
    )
    out_specs = (
        P("dp", "seq", None),
        P("dp", "seq", None),
        P("seq", "dp", None),
        P("seq", "dp", None),
    )
    body = functools.partial(shards, mesh.shape["seq"], mesh.shape["dp"])
    return jax.shard_map(body, mesh=mesh, in_specs=in_specs, out_specs=out_specs, check_vma=False)
```
